256 devices in a mesh: sect: 2 (over core), blk: 128 (over x, z, y).
Axes of the slice: x: 4, y: 4, z: 8, core: 2. Of those that a mesh axis runs over, the one named last changes fastest.
Arguments:
- start_remainders: bfloat16 [2, 128, 256, 256], P(None, 'blk'), may hold values from -6 to 6
- site_tensors: bfloat16 [4, 128, 4, 256, 256], P('sect', 'blk'), may hold values from -0.375 to 0.375
- mpo_coeffs: float32 [4, 4], P('sect'), may hold values from 0.25 to 2
- mpo_pattern: int32 [4, 4], P('sect'), may hold values 0 or 1
- joining: int32 [4, 4, 128], P('sect'), may hold values from 0 to 127, each once within a row
- sector_dims: int32 [4, 128], P('sect'), may hold values from 64 to 256, as said below
Outputs:
- segment_remainders: bfloat16 [2, 2, 128, 256, 256], P('sect', None, 'blk')
The draws below stay inside these ranges and needn't reach their ends.
Inputs may be any that keep to these rules, and one draw needn't show every extreme that they name: Every joining[k, s] is a permutation of the 128 sectors. `sector_dims`: at every site some sector has the full size 256.
All inputs are finite; a program needn't handle non-finite values. No bound on the sum of `mpo_pattern` on one device may be relied on, other than what follows from the above.
Results may differ from the reference program's by a relative error of at most 0.009.
Values may be sent and summed in bfloat16 or wider, within the bound.
A program may use at most 64 MiB of HBM per device.

```python
import math
import jax
import jax.numpy as jnp
from jax import lax

B = 256
D_PHYS = 4
SITE_SEC = 2
MICRO = 2
NSEC = 128
SITES = 4


def draw_sector_dims(key, part):
    sizes = jax.random.randint(key, (SITES, NSEC), B // 4, B + 1)
    chosen = jax.random.randint(jax.random.fold_in(key, 7), (SITES,), 0, NSEC)
    positions = jnp.arange(NSEC)
    return jnp.where(positions[None, :] == chosen[:, None], B, sizes).astype(jnp.int32)


def plant(entries, key, low, high):
    shape = entries.shape
    spot = [jax.random.randint(jax.random.fold_in(key, axis), (), 0, shape[axis]) for axis in range(len(shape))]
    entries = entries.at[tuple(spot)].set(low)
    longest = shape.index(max(shape))
    spot[longest] = (spot[longest] + 1) % shape[longest]
    return entries.at[tuple(spot)].set(high)


def block_scale(rng, shape, shards, least, high):
    gain, own = 1.0, jax.random.fold_in(rng, 6)
    for position, parts in shards:
        heights = jnp.exp(jax.random.uniform(jax.random.fold_in(own, position), (parts,), jnp.float32, least / len(shards), high / len(shards)))
        gain = gain * jnp.repeat(heights, shape[position] // parts).reshape([-1 if axis == position else 1 for axis in range(len(shape))])
    return gain


def centred(rng, extent, deviation, reach, shards=(), kind=jnp.bfloat16):
    drawn = deviation * jax.random.normal(rng, extent, jnp.float32)
    if shards:
        drawn = drawn * block_scale(rng, extent, shards, -0.22, 0.18)
    return jnp.clip(drawn, -reach, reach).astype(kind)


def setup_inputs(seed: int = 0) -> dict:
    streams_of = jax.random.split(jax.random.key(seed), 7)
    return {
        "start_remainders": centred(streams_of[0], (MICRO, NSEC, B, B), 1.0, 6.0, ((1, 128),)),
        "site_tensors": centred(streams_of[1], (SITES, NSEC, D_PHYS, B, B), B ** -0.5, 0.375, ((0, 2), (1, 128))),
        "mpo_coeffs": jnp.clip(jnp.exp(math.log(2.0) - 2.0794415 * jax.random.uniform(streams_of[2], (SITES, D_PHYS), jnp.float32) ** block_scale(streams_of[2], (SITES, D_PHYS), ((0, 2),), -0.2, 0.2)), 0.25, 2.0),
        "mpo_pattern": plant((jax.random.randint(streams_of[3], (SITES, D_PHYS), 0, 4) < 3).astype(jnp.int32), jax.random.fold_in(streams_of[3], 1), 0, 1),
        "joining": jax.vmap(lambda own: jax.random.permutation(own, NSEC))(jax.random.split(streams_of[4], SITES * D_PHYS)).reshape((SITES, D_PHYS, NSEC)).astype(jnp.int32),
        "sector_dims": draw_sector_dims(jax.random.fold_in(streams_of[6], 71), 0),
    }


def advance(blocks, tensor, channel_weight, inverse, live_sizes):
    widened = blocks.astype(jnp.float32)
    summed = jnp.zeros(blocks.shape, jnp.float32)
    for phys in range(D_PHYS):
        product = jnp.einsum('aij,ajl->ail', widened, tensor[:, phys].astype(jnp.float32)).astype(jnp.bfloat16)
        summed = summed + channel_weight[phys] * jnp.take(product, inverse[phys], axis=0).astype(jnp.float32)
    indices = jnp.arange(B, dtype=jnp.int32)
    live_mask = (indices[None, :, None] < live_sizes[:, None, None]) & (indices[None, None, :] < live_sizes[:, None, None])
    grouped = lax.optimization_barrier(jnp.where(live_mask, summed, 0.0).astype(jnp.bfloat16)).astype(jnp.float32)
    meansq = lax.optimization_barrier(jnp.mean(grouped * grouped, axis=(1, 2), keepdims=True))
    return (grouped * lax.rsqrt(meansq + 1e-06)).astype(jnp.bfloat16)

def reference(start_remainders, site_tensors, mpo_coeffs, mpo_pattern, joining, sector_dims):
    channel_weight = mpo_coeffs * mpo_pattern.astype(jnp.float32)
    inverse = jnp.argsort(joining, axis=-1).astype(jnp.int32)
    remainder = start_remainders
    collected = []
    for site in range(SITES):
        remainder = lax.map(lambda blocks: advance(blocks, site_tensors[site], channel_weight[site], inverse[site], sector_dims[site]), remainder)
        if (site + 1) % SITE_SEC == 0:
            collected.append(remainder)
    return jnp.stack(collected)
```

```python
import functools

import jax
import jax.numpy as jnp
from jax import lax
from jax.experimental import pallas as pl
from jax.experimental.pallas import tpu as pltpu
from jax.sharding import PartitionSpec as P

MESH = pl.DeviceIdType.MESH
B = 256
PHYS = 4
SITES = 4
CHIPS = 128
HUBS = 64
ROWS, COLS = 8, 128


def far_first(step):
    half, sign = (step + 1) // 2, 1 - 2 * (step % 2)
    return (12 + sign * half) % 8


def kernel(
    start_ref, tensor_ref, inverse_ref, dims_ref, weight_ref, out_ref,
    tensors, remainder, parting, made, gathered_even, gathered_odd, joined, returned,
    tensor_sems, made_send, made_recv, joined_send, joined_recv, own_sem, part_sems,
):
    me, state = lax.axis_index("blk"), lax.axis_index("sect")
    x, z, y = me // 32, (me // 4) % 8, me % 4
    is_hub = me % 2 == state
    tile = me // 2
    sibling = {"sect": 1 - state}
    across = [((x + i) % 4) * 32 for i in (2, 1, 3, 0)]
    along = [(y + i) % 4 for i in (2, 1, 3, 0)]
    hub_along = [((y // 2 + i) % 2) * 2 + state for i in (1, 0)]

    def layer(step):
        return ((z + far_first(step)) % 8) * 4

    barrier = pltpu.get_barrier_semaphore()

    def greet(chip):
        pl.semaphore_signal(barrier, inc=1, device_id={"blk": chip}, device_id_type=MESH)

    pl.semaphore_signal(barrier, inc=1, device_id=sibling, device_id_type=MESH)

    def each_chip(visit):
        def body(step, carry):
            base = layer(step)
            for i in range(4):
                for j in range(4):
                    chip = base + across[i] + along[j]
                    visit(chip, i == 3 and j == 3)
            return carry

        lax.fori_loop(0, 8, body, 0)

    def each_hub(visit):
        def body(step, carry):
            base = layer(step)
            for i in range(4):
                for j in range(2):
                    chip = base + across[i] + hub_along[j]
                    visit(chip, i == 3)
            return carry

        lax.fori_loop(0, 8, body, 0)

    def greet_other(chip, maybe_me):
        if maybe_me:
            pl.when(chip != me)(lambda: greet(chip))
        else:
            greet(chip)

    @pl.when(is_hub)
    def _():
        each_chip(greet_other)

    @pl.when(jnp.logical_not(is_hub))
    def _():
        each_hub(greet_other)

    start_copy = pltpu.make_async_copy(start_ref.at[state], remainder, own_sem.at[1])
    start_copy.start()

    def own_tensor(j):
        return pltpu.make_async_copy(tensor_ref.at[j], tensors.at[state * 2 + j], tensor_sems.at[0, j])

    def sent_tensor(j, slot):
        return pltpu.make_async_remote_copy(
            tensor_ref.at[j], tensors.at[slot * 2 + j], tensor_sems.at[1, j], tensor_sems.at[2, j],
            device_id=sibling, device_id_type=MESH,
        )

    for j in range(2):
        own_tensor(j).start()
    start_copy.wait()

    @pl.when(is_hub)
    def _():
        pl.semaphore_wait(barrier, CHIPS)

    @pl.when(jnp.logical_not(is_hub))
    def _():
        pl.semaphore_wait(barrier, HUBS + 1)

    for j in range(2):
        sent_tensor(j, state).start()

    row_ids = (tile // 2) * ROWS + lax.broadcasted_iota(jnp.int32, (ROWS, COLS), 0)
    col_ids = (tile % 2) * COLS + lax.broadcasted_iota(jnp.int32, (ROWS, COLS), 1)

    def site_step(site, gathered):
        @pl.when(site // 2 == state)
        def _():
            own_tensor(site % 2).wait()

        @pl.when(site // 2 != state)
        def _():
            sent_tensor(site % 2, 1 - state).wait_recv()

        for phys in range(PHYS):
            product = jnp.dot(remainder[...], tensors[site, phys], preferred_element_type=jnp.float32)
            for side in range(2):
                part = product[:, side * COLS : (side + 1) * COLS].reshape(B // ROWS, ROWS, COLS)
                made[site, :, side, phys] = part.astype(jnp.bfloat16)

        def send_made(chip, maybe_me):
            there = chip // 2

            def go():
                pltpu.make_async_remote_copy(
                    made.at[site, there // 2, there % 2], gathered.at[me],
                    made_send.at[site], made_recv.at[site],
                    device_id={"blk": chip}, device_id_type=MESH,
                ).start()

            if maybe_me:
                pl.when(chip != me)(go)
            else:
                go()

        each_hub(send_made)

        @pl.when(is_hub)
        def _():
            own = pltpu.make_async_copy(made.at[site, tile // 2, tile % 2], gathered.at[me], own_sem.at[0])
            own.start()
            own.wait()
            pltpu.make_async_remote_copy(
                gathered.at[pl.ds(0, CHIPS - 1)], gathered.at[pl.ds(0, CHIPS - 1)],
                made_send.at[site], made_recv.at[site], device_id=sibling, device_id_type=MESH,
            ).wait_recv()
            weights = [weight_ref[site * PHYS + phys] for phys in range(PHYS)]

            def join(chip, maybe_me):
                total = jnp.zeros((ROWS, COLS), jnp.float32)
                for phys in range(PHYS):
                    left = inverse_ref[site * PHYS + phys, chip]
                    total = total + weights[phys] * gathered[left, phys].astype(jnp.float32)
                size = dims_ref[site, chip]
                total = jnp.where((row_ids < size) & (col_ids < size), total, 0.0)
                joined[site, chip] = total.astype(jnp.bfloat16)

                def go():
                    pltpu.make_async_remote_copy(
                        joined.at[site, chip], returned.at[site, tile],
                        joined_send.at[site], joined_recv.at[site],
                        device_id={"blk": chip}, device_id_type=MESH,
                    ).start()

                def keep():
                    own = pltpu.make_async_copy(joined.at[site, chip], returned.at[site, tile], own_sem.at[0])
                    own.start()
                    own.wait()

                if maybe_me:
                    pl.when(chip != me)(go)
                    pl.when(chip == me)(keep)
                else:
                    go()

            each_chip(join)

        def arrive(count):
            pltpu.make_async_remote_copy(
                returned.at[site, pl.ds(0, count)], returned.at[site, pl.ds(0, count)],
                joined_send.at[site], joined_recv.at[site], device_id=sibling, device_id_type=MESH,
            ).wait_recv()

        @pl.when(is_hub)
        def _():
            arrive(HUBS - 1)

        @pl.when(jnp.logical_not(is_hub))
        def _():
            arrive(HUBS)

        tiles = returned[site].astype(jnp.float32)
        squares = jnp.sum(tiles * tiles, axis=0)
        meansq = jnp.sum(squares, keepdims=True) * (1.0 / (B * B))
        scale = lax.rsqrt(meansq + 1e-06)
        tiles = (tiles * scale[None]).reshape(B // ROWS, 2, ROWS, COLS)
        for side in range(2):
            remainder[:, side * COLS : (side + 1) * COLS] = tiles[:, side].reshape(B, COLS).astype(jnp.bfloat16)

        @pl.when((site % 2 == 1) & (site // 2 == state))
        def _():
            out_ref[state] = remainder[...]

        @pl.when((site % 2 == 1) & (site // 2 != state))
        def _():
            parting[...] = remainder[...]
            part_copy(state).start()

    def part_copy(slot):
        return pltpu.make_async_remote_copy(
            parting, out_ref.at[slot], part_sems.at[0], part_sems.at[1],
            device_id=sibling, device_id_type=MESH,
        )

    def section_step(section, carry):
        site_step(section * 2, gathered_even)
        site_step(section * 2 + 1, gathered_odd)
        return carry

    lax.fori_loop(0, SITES // 2, section_step, 0)

    part_copy(1 - state).wait_recv()
    part_copy(state).wait_send()
    for j in range(2):
        sent_tensor(j, state).wait_send()

    def settle(site, carry):
        def left_made(count):
            pltpu.make_async_remote_copy(
                gathered_even.at[pl.ds(0, count)], gathered_even.at[pl.ds(0, count)],
                made_send.at[site], made_recv.at[site], device_id=sibling, device_id_type=MESH,
            ).wait_send()

        @pl.when(is_hub)
        def _():
            left_made(HUBS - 1)
            pltpu.make_async_remote_copy(
                joined.at[site, pl.ds(0, CHIPS - 1)], joined.at[site, pl.ds(0, CHIPS - 1)],
                joined_send.at[site], joined_recv.at[site], device_id=sibling, device_id_type=MESH,
            ).wait_send()

        @pl.when(jnp.logical_not(is_hub))
        def _():
            left_made(HUBS)

        return carry

    lax.fori_loop(0, SITES, settle, 0)


def shards(start_remainders, site_tensors, mpo_coeffs, mpo_pattern, joining, sector_dims):
    channel_weight = mpo_coeffs * mpo_pattern.astype(jnp.float32)
    sectors = jnp.arange(CHIPS, dtype=jnp.int32)
    hit = joining[:, :, :, None] == sectors[None, None, None, :]
    inverse = jnp.sum(jnp.where(hit, sectors[None, None, :, None], 0), axis=2, dtype=jnp.int32)
    table = jnp.concatenate([inverse, sector_dims[:, None, :]], axis=1)

    def both(block):
        other = lax.ppermute(block, "sect", [(0, 1), (1, 0)])
        first = lax.axis_index("sect") == 0
        return jnp.concatenate([jnp.where(first, block, other), jnp.where(first, other, block)], axis=0)

    table, channel_weight = both(table), both(channel_weight)
    bf16, dma = jnp.bfloat16, pltpu.SemaphoreType.DMA
    out = pl.pallas_call(
        kernel,
        out_shape=jax.ShapeDtypeStruct((2, B, B), bf16),
        in_specs=[
            pl.BlockSpec(memory_space=pl.ANY),
            pl.BlockSpec(memory_space=pl.ANY),
            pl.BlockSpec(memory_space=pltpu.SMEM),
            pl.BlockSpec(memory_space=pltpu.SMEM),
            pl.BlockSpec(memory_space=pltpu.SMEM),
        ],
        out_specs=pl.BlockSpec(memory_space=pltpu.VMEM),
        scratch_shapes=[
            pltpu.VMEM((SITES, PHYS, B, B), bf16),
            pltpu.VMEM((B, B), bf16),
            pltpu.VMEM((B, B), bf16),
            pltpu.VMEM((SITES, B // ROWS, 2, PHYS, ROWS, COLS), bf16),
            pltpu.VMEM((CHIPS, PHYS, ROWS, COLS), bf16),
            pltpu.VMEM((CHIPS, PHYS, ROWS, COLS), bf16),
            pltpu.VMEM((SITES, CHIPS, ROWS, COLS), bf16),
            pltpu.VMEM((SITES, HUBS, ROWS, COLS), bf16),
            dma((3, 2)),
            dma((SITES,)),
            dma((SITES,)),
            dma((SITES,)),
            dma((SITES,)),
            dma((2,)),
            dma((2,)),
        ],
        compiler_params=pltpu.CompilerParams(
            collective_id=0, has_side_effects=True, vmem_limit_bytes=40 << 20
        ),
        name="zip_up",
    )(
        start_remainders[:, 0],
        site_tensors[:, 0],
        table[:, :PHYS].reshape(SITES * PHYS, CHIPS),
        table[:, PHYS],
        channel_weight.reshape(SITES * PHYS),
    )
    return out[None, :, None]


def solution(mesh):
    in_specs = (
        P(None, "blk", None, None),
        P("sect", "blk", None, None, None),
        P("sect", None),
        P("sect", None),
        P("sect", None, None),
        P("sect", None),
    )
    out_specs = P("sect", None, "blk", None, None)
    return jax.shard_map(shards, mesh=mesh, in_specs=in_specs, out_specs=out_specs, check_vma=False)
```

```python
import jax
import jax.numpy as jnp
from jax import lax
from jax.experimental import pallas as pl
from jax.experimental.pallas import tpu as pltpu
from jax.sharding import PartitionSpec as P

MESH = pl.DeviceIdType.MESH
B = 256
PHYS = 4
SITES = 4
CHIPS = 128
TILES = 64
ROWS, COLS = 8, 128
OFFSETS = [(i, j) for i in (2, 1, 3, 0) for j in (2, 1, 3, 0)]


def far_first(step):
    half, sign = (step + 1) // 2, 1 - 2 * (step % 2)
    return (12 + sign * half) % 8


def kernel(
    start_ref, tensor_ref, coeff_ref, pattern_ref, joining_ref, dims_ref, out_ref,
    coeffs, pattern, joining, tables, weights_all, lookup,
    tensors, remainder, parting, made, gathered_even, gathered_odd, joined, returned,
    tensor_sems, made_send, made_recv, joined_send, joined_recv, own_sem, part_sems, table_sems, small_sems,
):
    me, state = lax.axis_index("blk"), lax.axis_index("sect")
    x, z, y = me // 32, (me // 4) % 8, me % 4
    sibling = {"sect": 1 - state}
    tile = (x * 4 + z % 4) * 4 + y
    half = z // 4
    xs = [(x + i) % 4 for i in range(4)]
    ys = [(y + i) % 4 for i in range(4)]

    def each_chip(visit):
        def body(step, carry):
            base = ((z + far_first(step)) % 8) * 4
            for i, j in OFFSETS:
                visit(base + xs[i] * 32 + ys[j], i == 0 and j == 0)
            return carry

        lax.fori_loop(0, 8, body, 0)

    def each_hub(visit):
        for i, j in OFFSETS:
            hub_z = (z + 2 + 4 * ((xs[i] + ys[j]) % 2)) % 8
            visit(xs[i], hub_z, ys[j], False)

        def body(step, carry):
            hub_z = (z + 7 + (step + 1) % 3) % 8
            for i, j in OFFSETS:
                visit(xs[i], hub_z, ys[j], i == 0 and j == 0)
            return carry

        lax.fori_loop(1, 4, body, 0)

    def unless_me(chip, maybe_me, go):
        if maybe_me:
            pl.when(chip != me)(go)
        else:
            go()

    barrier = pltpu.get_barrier_semaphore()
    pl.semaphore_signal(barrier, inc=1, device_id=sibling, device_id_type=MESH)

    def greet(chip, maybe_me):
        unless_me(
            chip, maybe_me,
            lambda: pl.semaphore_signal(barrier, inc=1, device_id={"blk": chip}, device_id_type=MESH),
        )

    each_chip(greet)

    start_copy = pltpu.make_async_copy(start_ref.at[state], remainder, own_sem.at[1])
    start_copy.start()

    def own_tensor(j):
        return pltpu.make_async_copy(tensor_ref.at[j], tensors.at[state * 2 + j], tensor_sems.at[0, j])

    def sent_tensor(j, slot):
        return pltpu.make_async_remote_copy(
            tensor_ref.at[j], tensors.at[slot * 2 + j], tensor_sems.at[1, j], tensor_sems.at[2, j],
            device_id=sibling, device_id_type=MESH,
        )

    for j in range(2):
        own_tensor(j).start()
    small_copies = [
        pltpu.make_async_copy(source, target, small_sems.at[i])
        for i, (source, target) in enumerate(
            [
                (joining_ref, joining),
                (dims_ref, tables.at[state, pl.ds(2 * PHYS, 2)]),
                (coeff_ref, coeffs),
                (pattern_ref, pattern),
            ]
        )
    ]
    for copy in small_copies:
        copy.start()

    for i in range(4):
        away = (z + 3 + i) % 8 if i < 3 else (z + 2 + 4 * ((x + y + 1) % 2) + 4) % 8
        for column in range(4):
            slots = pl.ds(column * 32 + away * 4, 4)
            gathered_even[slots] = jnp.zeros((4, PHYS, ROWS, COLS), jnp.bfloat16)
            gathered_odd[slots] = jnp.zeros((4, PHYS, ROWS, COLS), jnp.bfloat16)

    for copy in small_copies:
        copy.wait()

    turned = jnp.concatenate([joining[...], jnp.zeros((CHIPS - 2 * PHYS, CHIPS), jnp.int32)], axis=0).T
    left_ids = lax.broadcasted_iota(jnp.int32, (CHIPS, CHIPS), 0)
    right_ids = lax.broadcasted_iota(jnp.int32, (CHIPS, CHIPS), 1)
    for row in range(2 * PHYS):
        hit = jnp.where(turned[:, row : row + 1] == right_ids, left_ids, 0)
        tables[state, row : row + 1] = jnp.max(hit, axis=0, keepdims=True)
    weights_all[state, :, :PHYS] = coeffs[...] * pattern[...].astype(jnp.float32)

    def sent_table(slot):
        return pltpu.make_async_remote_copy(
            tables.at[slot], tables.at[slot], table_sems.at[0], table_sems.at[1],
            device_id=sibling, device_id_type=MESH,
        )

    def sent_weights(slot):
        return pltpu.make_async_remote_copy(
            weights_all.at[slot], weights_all.at[slot], table_sems.at[2], table_sems.at[3],
            device_id=sibling, device_id_type=MESH,
        )

    lookup_copy = pltpu.make_async_copy(tables, lookup, table_sems.at[4])
    start_copy.wait()
    pl.semaphore_wait(barrier, CHIPS)

    for j in range(2):
        sent_tensor(j, state).start()
    sent_table(state).start()
    sent_weights(state).start()

    row_ids = (tile // 2) * ROWS + lax.broadcasted_iota(jnp.int32, (ROWS, COLS), 0)
    col_ids = (tile % 2) * COLS + lax.broadcasted_iota(jnp.int32, (ROWS, COLS), 1)

    def all_made(site):
        slots = pl.ds(0, TILES - 1)
        return pltpu.make_async_remote_copy(
            gathered_even.at[slots], gathered_even.at[slots], made_send.at[site], made_recv.at[site],
            device_id=sibling, device_id_type=MESH,
        )

    def all_joined(site):
        slots = pl.ds(0, CHIPS - 1)
        return pltpu.make_async_remote_copy(
            joined.at[site, slots], joined.at[site, slots], joined_send.at[site], joined_recv.at[site],
            device_id=sibling, device_id_type=MESH,
        )

    def part_copy(slot):
        return pltpu.make_async_remote_copy(
            parting, out_ref.at[slot], part_sems.at[0], part_sems.at[1],
            device_id=sibling, device_id_type=MESH,
        )

    def site_step(section, row, gathered):
        site = section * 2 + row

        @pl.when(section == state)
        def _():
            own_tensor(row).wait()

        @pl.when(section != state)
        def _():
            sent_tensor(row, 1 - state).wait_recv()

        for phys in range(PHYS):
            product = jnp.dot(remainder[...], tensors[site, phys], preferred_element_type=jnp.float32)
            for side in range(2):
                part = product[:, side * COLS : (side + 1) * COLS].reshape(B // ROWS, ROWS, COLS)
                made[site, :, side, phys] = part.astype(jnp.bfloat16)

        def send_made(hub_x, hub_z, hub_y, maybe_me):
            chip = hub_x * 32 + hub_z * 4 + hub_y
            there = (hub_x * 4 + hub_z % 4) * 4 + hub_y

            def go():
                pltpu.make_async_remote_copy(
                    made.at[site, there // 2, there % 2], gathered.at[me],
                    made_send.at[site], made_recv.at[site],
                    device_id={"blk": chip}, device_id_type=MESH,
                ).start()

            unless_me(chip, maybe_me, go)

        each_hub(send_made)
        own = pltpu.make_async_copy(made.at[site, tile // 2, tile % 2], gathered.at[me], own_sem.at[0])
        own.start()

        if row == 0:
            @pl.when(section == 0)
            def _():
                sent_table(1 - state).wait_recv()
                sent_weights(1 - state).wait_recv()
                lookup_copy.start()
                lookup_copy.wait()

        own.wait()
        all_made(site).wait_recv()
        weight_row = weights_all[section, row : row + 1]
        weights = [weight_row[:, phys : phys + 1] for phys in range(PHYS)]

        def join(chip, maybe_me):
            total = jnp.zeros((ROWS, COLS), jnp.float32)
            for phys in range(PHYS):
                left = lookup[section, row * PHYS + phys, chip]
                total = total + weights[phys] * gathered[left, phys].astype(jnp.float32)
            size = lookup[section, 2 * PHYS + row, chip]
            total = jnp.where((row_ids < size) & (col_ids < size), total, 0.0)
            joined[site, chip] = total.astype(jnp.bfloat16)

            def go():
                pltpu.make_async_remote_copy(
                    joined.at[site, chip], returned.at[site, half, tile],
                    joined_send.at[site], joined_recv.at[site],
                    device_id={"blk": chip}, device_id_type=MESH,
                ).start()

            unless_me(chip, maybe_me, go)

        each_chip(join)
        own = pltpu.make_async_copy(joined.at[site, me], returned.at[site, half, tile], own_sem.at[0])
        own.start()
        own.wait()
        all_joined(site).wait_recv()

        tiles = returned[site, 0].astype(jnp.float32) + returned[site, 1].astype(jnp.float32)
        squares = jnp.sum(tiles * tiles, axis=0)
        meansq = jnp.sum(squares, keepdims=True) * (1.0 / (B * B))
        scale = lax.rsqrt(meansq + 1e-06)
        tiles = (tiles * scale[None]).reshape(B // ROWS, 2, ROWS, COLS)
        for side in range(2):
            remainder[:, side * COLS : (side + 1) * COLS] = tiles[:, side].reshape(B, COLS).astype(jnp.bfloat16)

        if row == 1:
            @pl.when(section == state)
            def _():
                out_ref[state] = remainder[...]

            @pl.when(section != state)
            def _():
                parting[...] = remainder[...]
                part_copy(state).start()

    def section_step(section, carry):
        site_step(section, 0, gathered_even)
        site_step(section, 1, gathered_odd)
        return carry

    lax.fori_loop(0, SITES // 2, section_step, 0)

    for j in range(2):
        sent_tensor(j, state).wait_send()
    sent_table(state).wait_send()
    sent_weights(state).wait_send()

    def settle(site, carry):
        all_made(site).wait_send()
        all_joined(site).wait_send()
        return carry

    lax.fori_loop(0, SITES, settle, 0)
    part_copy(state).wait_send()
    part_copy(1 - state).wait_recv()


def shards(start_remainders, site_tensors, mpo_coeffs, mpo_pattern, joining, sector_dims):
    bf16, dma = jnp.bfloat16, pltpu.SemaphoreType.DMA
    out = pl.pallas_call(
        kernel,
        out_shape=jax.ShapeDtypeStruct((2, B, B), bf16),
        in_specs=[pl.BlockSpec(memory_space=pltpu.HBM)] * 6,
        out_specs=pl.BlockSpec(memory_space=pltpu.VMEM),
        scratch_shapes=[
            pltpu.VMEM((2, PHYS), jnp.float32),
            pltpu.VMEM((2, PHYS), jnp.int32),
            pltpu.VMEM((2 * PHYS, CHIPS), jnp.int32),
            pltpu.VMEM((2, 16, CHIPS), jnp.int32),
            pltpu.VMEM((2, 2, CHIPS), jnp.float32),
            pltpu.SMEM((2, 16, CHIPS), jnp.int32),
            pltpu.VMEM((SITES, PHYS, B, B), bf16),
            pltpu.VMEM((B, B), bf16),
            pltpu.VMEM((B, B), bf16),
            pltpu.VMEM((SITES, B // ROWS, 2, PHYS, ROWS, COLS), bf16),
            pltpu.VMEM((CHIPS, PHYS, ROWS, COLS), bf16),
            pltpu.VMEM((CHIPS, PHYS, ROWS, COLS), bf16),
            pltpu.VMEM((SITES, CHIPS, ROWS, COLS), bf16),
            pltpu.VMEM((SITES, 2, TILES, ROWS, COLS), bf16),
            dma((3, 2)),
            dma((SITES,)),
            dma((SITES,)),
            dma((SITES,)),
            dma((SITES,)),
            dma((2,)),
            dma((2,)),
            dma((5,)),
            dma((4,)),
        ],
        compiler_params=pltpu.CompilerParams(
            collective_id=0, has_side_effects=True, vmem_limit_bytes=63 << 20
        ),
        name="zip_up",
    )(
        start_remainders[:, 0],
        site_tensors[:, 0],
        mpo_coeffs,
        mpo_pattern,
        joining.reshape(2 * PHYS, CHIPS),
        sector_dims,
    )
    return out[None, :, None]


def solution(mesh):
    in_specs = (
        P(None, "blk", None, None),
        P("sect", "blk", None, None, None),
        P("sect", None),
        P("sect", None),
        P("sect", None, None),
        P("sect", None),
    )
    out_specs = P("sect", None, "blk", None, None)
    return jax.shard_map(shards, mesh=mesh, in_specs=in_specs, out_specs=out_specs, check_vma=False)
```

```python
import jax
import jax.numpy as jnp
from jax import lax
from jax.experimental import pallas as pl
from jax.experimental.pallas import tpu as pltpu
from jax.sharding import PartitionSpec as P

MESH = pl.DeviceIdType.MESH
B = 256
PHYS = 4
SITES = 4
CHIPS = 128
TILES = 64
ROWS, COLS = 8, 128
def hops(d):
    return min(d // 32, 4 - d // 32) + min(d // 4 % 8, 8 - d // 4 % 8) + min(d % 4, 4 - d % 4)


ORDER = sorted(range(CHIPS), key=lambda d: (-hops(d), d * 37 % CHIPS))
NEAR = [d for d in ORDER if 0 < hops(d) <= 4]


def nearer_hubs():
    chosen = []
    for d in range(CHIPS):
        opposite = (d // 32 + 2) % 4 * 32 + (d // 4 % 8 + 4) % 8 * 4 + (d % 4 + 2) % 4
        here, there = [(hops(e), min(e // 4 % 8, 8 - e // 4 % 8)) for e in (d, opposite)]
        tie = here == there and d in (10, 26, 41, 59, 107, 121)
        if here < there or tie:
            chosen.append(d)
    return [d for d in ORDER if d in chosen]


HUBS = nearer_hubs()


def kernel(
    start_ref, tensor_ref, coeff_ref, pattern_ref, joining_ref, dims_ref, out_ref,
    coeffs, pattern, joining, tables, weights_all, lookup,
    tensors, remainder, parting, made, gathered_even, gathered_odd, joined, returned,
    tensor_sems, made_send, made_recv, joined_send, joined_recv, own_sem, part_sems, table_sems, small_sems,
):
    me, state = lax.axis_index("blk"), lax.axis_index("sect")
    x, z, y = me // 32, (me // 4) % 8, me % 4
    sibling = {"sect": 1 - state}
    half = z // 4
    tile = ((x + 2 * half) % 4 * 4 + z % 4) * 4 + (y + 2 * half) % 4
    xs = [(x + i) % 4 for i in range(4)]
    zs = [(z + i) % 8 for i in range(8)]
    ys = [(y + i) % 4 for i in range(4)]

    def at(d):
        return xs[d // 32] * 32 + zs[d // 4 % 8] * 4 + ys[d % 4]

    barrier = pltpu.get_barrier_semaphore()
    pl.semaphore_signal(barrier, inc=1, device_id=sibling, device_id_type=MESH)

    for d in NEAR:
        pl.semaphore_signal(barrier, inc=1, device_id={"blk": at(d)}, device_id_type=MESH)

    start_copy = pltpu.make_async_copy(start_ref.at[state], remainder, own_sem.at[1])
    start_copy.start()

    def own_tensor(j):
        return pltpu.make_async_copy(tensor_ref.at[j], tensors.at[state * 2 + j], tensor_sems.at[0, j])

    def sent_tensor(j, slot):
        return pltpu.make_async_remote_copy(
            tensor_ref.at[j], tensors.at[slot * 2 + j], tensor_sems.at[1, j], tensor_sems.at[2, j],
            device_id=sibling, device_id_type=MESH,
        )

    for j in range(2):
        own_tensor(j).start()
    small_copies = [
        pltpu.make_async_copy(source, target, small_sems.at[i])
        for i, (source, target) in enumerate(
            [
                (joining_ref, joining),
                (dims_ref, tables.at[state, pl.ds(2 * PHYS, 2)]),
                (coeff_ref, coeffs),
                (pattern_ref, pattern),
            ]
        )
    ]
    for copy in small_copies:
        copy.start()

    for d in range(CHIPS):
        if d not in HUBS:
            slot = at((4 - d // 32) % 4 * 32 + (8 - d // 4 % 8) % 8 * 4 + (4 - d % 4) % 4)
            gathered_even[slot] = jnp.zeros((PHYS, ROWS, COLS), jnp.bfloat16)
            gathered_odd[slot] = jnp.zeros((PHYS, ROWS, COLS), jnp.bfloat16)

    for copy in small_copies:
        copy.wait()

    turned = jnp.concatenate([joining[...], jnp.zeros((CHIPS - 2 * PHYS, CHIPS), jnp.int32)], axis=0).T
    left_ids = lax.broadcasted_iota(jnp.int32, (CHIPS, CHIPS), 0)
    right_ids = lax.broadcasted_iota(jnp.int32, (CHIPS, CHIPS), 1)
    for row in range(2 * PHYS):
        hit = jnp.where(turned[:, row : row + 1] == right_ids, left_ids, 0)
        tables[state, row : row + 1] = jnp.max(hit, axis=0, keepdims=True)
    weights_all[state, :, :PHYS] = coeffs[...] * pattern[...].astype(jnp.float32)

    def sent_table(slot):
        return pltpu.make_async_remote_copy(
            tables.at[slot], tables.at[slot], table_sems.at[0], table_sems.at[1],
            device_id=sibling, device_id_type=MESH,
        )

    def sent_weights(slot):
        return pltpu.make_async_remote_copy(
            weights_all.at[slot], weights_all.at[slot], table_sems.at[2], table_sems.at[3],
            device_id=sibling, device_id_type=MESH,
        )

    lookup_copy = pltpu.make_async_copy(tables, lookup, table_sems.at[4])
    start_copy.wait()
    pl.semaphore_wait(barrier, len(NEAR) + 1)

    for j in range(2):
        sent_tensor(j, state).start()
    sent_table(state).start()
    sent_weights(state).start()

    row_ids = (tile // 2) * ROWS + lax.broadcasted_iota(jnp.int32, (ROWS, COLS), 0)
    col_ids = (tile % 2) * COLS + lax.broadcasted_iota(jnp.int32, (ROWS, COLS), 1)

    def all_made(site):
        slots = pl.ds(0, TILES - 1)
        return pltpu.make_async_remote_copy(
            gathered_even.at[slots], gathered_even.at[slots], made_send.at[site], made_recv.at[site],
            device_id=sibling, device_id_type=MESH,
        )

    def all_joined(site):
        slots = pl.ds(0, CHIPS - 1)
        return pltpu.make_async_remote_copy(
            joined.at[0, slots], joined.at[0, slots], joined_send.at[site], joined_recv.at[site],
            device_id=sibling, device_id_type=MESH,
        )

    def part_copy():
        return pltpu.make_async_remote_copy(
            parting, out_ref.at[1], part_sems.at[0], part_sems.at[1],
            device_id=sibling, device_id_type=MESH,
        )

    def site_step(section, row, gathered):
        site = section * 2 + row

        @pl.when(section == state)
        def _():
            own_tensor(row).wait()

        @pl.when(section != state)
        def _():
            sent_tensor(row, 1 - state).wait_recv()

        for phys in range(PHYS):
            product = jnp.dot(remainder[...], tensors[site, phys], preferred_element_type=jnp.float32)
            for side in range(2):
                part = product[:, side * COLS : (side + 1) * COLS].reshape(B // ROWS, ROWS, COLS)
                made[site, :, side, phys] = part.astype(jnp.bfloat16)

        for d in HUBS:
            if d:
                hub_half = zs[d // 4 % 8] // 4
                hub_tile = ((xs[d // 32] + 2 * hub_half) % 4 * 4 + zs[d // 4 % 8] % 4) * 4 + (ys[d % 4] + 2 * hub_half) % 4
                pltpu.make_async_remote_copy(
                    made.at[site, hub_tile // 2, hub_tile % 2], gathered.at[me],
                    made_send.at[site], made_recv.at[site],
                    device_id={"blk": at(d)}, device_id_type=MESH,
                ).start()
        own = pltpu.make_async_copy(made.at[site, tile // 2, tile % 2], gathered.at[me], own_sem.at[0])
        own.start()

        if row == 0:
            @pl.when(section == 0)
            def _():
                sent_table(1 - state).wait_recv()
                sent_weights(1 - state).wait_recv()
                lookup_copy.start()
                lookup_copy.wait()

        own.wait()
        all_made(site).wait_recv()
        weight_row = weights_all[section, row : row + 1]
        weights = [weight_row[:, phys : phys + 1] for phys in range(PHYS)]

        crossing = (1 - state) * section * row
        core, lane = state + crossing, site + crossing
        for d in ORDER:
            chip = at(d)
            total = jnp.zeros((ROWS, COLS), jnp.float32)
            for phys in range(PHYS):
                left = lookup[section, row * PHYS + phys, chip]
                total = total + weights[phys] * gathered[left, phys].astype(jnp.float32)
            size = lookup[section, 2 * PHYS + row, chip]
            total = jnp.where((row_ids < size) & (col_ids < size), total, 0.0)
            joined[site, chip] = total.astype(jnp.bfloat16)
            if d:
                pltpu.make_async_remote_copy(
                    joined.at[site, chip], returned.at[site, state, half, tile],
                    joined_send.at[lane], joined_recv.at[lane],
                    device_id={"sect": core, "blk": chip}, device_id_type=MESH,
                ).start()

        def finish(held):
            tiles = returned[site, held, 0].astype(jnp.float32) + returned[site, held, 1].astype(jnp.float32)
            squares = jnp.sum(tiles * tiles, axis=0)
            meansq = jnp.sum(squares, keepdims=True) * (1.0 / (B * B))
            scale = lax.rsqrt(meansq + 1e-06)
            tiles = (tiles * scale[None]).reshape(B // ROWS, 2, ROWS, COLS)
            for side in range(2):
                part = tiles[:, side].reshape(B, COLS).astype(jnp.bfloat16)
                remainder[:, side * COLS : (side + 1) * COLS] = part

        def to_sibling():
            return pltpu.make_async_remote_copy(
                joined.at[site, me], returned.at[site, state, half, tile],
                part_sems.at[2], part_sems.at[3], device_id=sibling, device_id_type=MESH,
            )

        def keep_own():
            own = pltpu.make_async_copy(joined.at[site, me], returned.at[site, state, half, tile], own_sem.at[0])
            own.start()
            own.wait()
            all_joined(site).wait_recv()
            finish(state)

        if row == 0:
            keep_own()
        else:
            @pl.when((section == 0) | (state == 1))
            def _():
                keep_own()

            @pl.when((section == 0) & (state == 0))
            def _():
                out_ref[0] = remainder[...]

            @pl.when((section == 0) & (state == 1))
            def _():
                parting[...] = remainder[...]
                part_copy().start()

            @pl.when((section == 1) & (state == 0))
            def _():
                to_sibling().start()
                to_sibling().wait_send()

            @pl.when((section == 1) & (state == 1))
            def _():
                out_ref[1] = remainder[...]
                to_sibling().wait_recv()
                all_joined(SITES).wait_recv()
                finish(0)
                out_ref[0] = remainder[...]

    def section_step(section, carry):
        site_step(section, 0, gathered_even)
        site_step(section, 1, gathered_odd)
        return carry

    lax.fori_loop(0, SITES // 2, section_step, 0)

    for j in range(2):
        sent_tensor(j, state).wait_send()
    sent_table(state).wait_send()
    sent_weights(state).wait_send()

    def settle(site, carry):
        all_made(site).wait_send()
        all_joined(site + (1 - state) * (site // (SITES - 1))).wait_send()
        return carry

    lax.fori_loop(0, SITES, settle, 0)

    @pl.when(state == 1)
    def _():
        part_copy().wait_send()

    @pl.when(state == 0)
    def _():
        part_copy().wait_recv()


def shards(start_remainders, site_tensors, mpo_coeffs, mpo_pattern, joining, sector_dims):
    bf16, dma = jnp.bfloat16, pltpu.SemaphoreType.DMA
    out = pl.pallas_call(
        kernel,
        out_shape=jax.ShapeDtypeStruct((2, B, B), bf16),
        in_specs=[pl.BlockSpec(memory_space=pltpu.HBM)] * 6,
        out_specs=pl.BlockSpec(memory_space=pltpu.VMEM),
        scratch_shapes=[
            pltpu.VMEM((2, PHYS), jnp.float32),
            pltpu.VMEM((2, PHYS), jnp.int32),
            pltpu.VMEM((2 * PHYS, CHIPS), jnp.int32),
            pltpu.VMEM((2, 16, CHIPS), jnp.int32),
            pltpu.VMEM((2, 2, CHIPS), jnp.float32),
            pltpu.SMEM((2, 16, CHIPS), jnp.int32),
            pltpu.VMEM((SITES, PHYS, B, B), bf16),
            pltpu.VMEM((B, B), bf16),
            pltpu.VMEM((B, B), bf16),
            pltpu.VMEM((SITES, B // ROWS, 2, PHYS, ROWS, COLS), bf16),
            pltpu.VMEM((CHIPS, PHYS, ROWS, COLS), bf16),
            pltpu.VMEM((CHIPS, PHYS, ROWS, COLS), bf16),
            pltpu.VMEM((SITES, CHIPS, ROWS, COLS), bf16),
            pltpu.VMEM((SITES, 2, 2, TILES, ROWS, COLS), bf16),
            dma((3, 2)),
            dma((SITES,)),
            dma((SITES,)),
            dma((SITES + 1,)),
            dma((SITES + 1,)),
            dma((2,)),
            dma((4,)),
            dma((5,)),
            dma((4,)),
        ],
        compiler_params=pltpu.CompilerParams(
            collective_id=0, has_side_effects=True, vmem_limit_bytes=63 << 20
        ),
        name="zip_up",
    )(
        start_remainders[:, 0],
        site_tensors[:, 0],
        mpo_coeffs,
        mpo_pattern,
        joining.reshape(2 * PHYS, CHIPS),
        sector_dims,
    )
    return out[None, :, None]


def solution(mesh):
    in_specs = (
        P(None, "blk", None, None),
        P("sect", "blk", None, None, None),
        P("sect", None),
        P("sect", None),
        P("sect", None, None),
        P("sect", None),
    )
    out_specs = P("sect", None, "blk", None, None)
    return jax.shard_map(shards, mesh=mesh, in_specs=in_specs, out_specs=out_specs, check_vma=False)
```

```python
import jax
import jax.numpy as jnp
from jax import lax
from jax.experimental import pallas as pl
from jax.experimental.pallas import tpu as pltpu
from jax.sharding import PartitionSpec as P

MESH = pl.DeviceIdType.MESH
B = 256
PHYS = 4
SITES = 4
CHIPS = 128
TILES = 64
ROWS, COLS = 8, 128
def hops(d):
    return min(d // 32, 4 - d // 32) + min(d // 4 % 8, 8 - d // 4 % 8) + min(d % 4, 4 - d % 4)


def alternate():
    chosen = []
    for d in sorted(range(CHIPS), key=lambda d: (-hops(d), d * 37 % CHIPS)):
        back = (4 - d // 32) % 4 * 32 + (8 - d // 4 % 8) % 8 * 4 + (4 - d % 4) % 4
        chosen += [e for e in (d, back) if e not in chosen]
    return [e for i, e in enumerate(chosen) if e not in chosen[:i]]


ORDER = alternate()
NEAR = [d for d in ORDER if 0 < hops(d) <= 4]


def nearer_hubs():
    chosen = []
    for d in range(CHIPS):
        opposite = (d // 32 + 2) % 4 * 32 + (d // 4 % 8 + 4) % 8 * 4 + (d % 4 + 2) % 4
        here, there = [(hops(e), min(e // 4 % 8, 8 - e // 4 % 8)) for e in (d, opposite)]
        tie = here == there and d in (10, 26, 41, 59, 107, 121)
        if here < there or tie:
            chosen.append(d)
    return [d for d in ORDER if d in chosen]


HUBS = nearer_hubs()


def kernel(
    start_ref, tensor_ref, coeff_ref, pattern_ref, joining_ref, dims_ref, out_ref,
    coeffs, pattern, joining, tables, weights_all, lookup,
    tensors, remainder, parting, made, gathered_even, gathered_odd, joined, returned,
    tensor_sems, made_send, made_recv, joined_send, joined_recv, own_sem, part_sems, table_sems, small_sems,
):
    me, state = lax.axis_index("blk"), lax.axis_index("sect")
    x, z, y = me // 32, (me // 4) % 8, me % 4
    sibling = {"sect": 1 - state}
    half = z // 4
    tile = ((x + 2 * half) % 4 * 4 + z % 4) * 4 + (y + 2 * half) % 4
    way = 1 - 2 * state
    xs = [(x + 4 + way * i) % 4 for i in range(4)]
    zs = [(z + 8 + way * i) % 8 for i in range(8)]
    ys = [(y + 4 + way * i) % 4 for i in range(4)]

    def at(d):
        return xs[d // 32] * 32 + zs[d // 4 % 8] * 4 + ys[d % 4]

    barrier = pltpu.get_barrier_semaphore()
    pl.semaphore_signal(barrier, inc=1, device_id=sibling, device_id_type=MESH)

    for d in NEAR:
        pl.semaphore_signal(barrier, inc=1, device_id={"blk": at(d)}, device_id_type=MESH)

    start_copy = pltpu.make_async_copy(start_ref.at[state], remainder, own_sem.at[1])
    start_copy.start()

    def own_tensor(j):
        return pltpu.make_async_copy(tensor_ref.at[j], tensors.at[state * 2 + j], tensor_sems.at[0, j])

    def sent_tensor(j, slot):
        return pltpu.make_async_remote_copy(
            tensor_ref.at[j], tensors.at[slot * 2 + j], tensor_sems.at[1, j], tensor_sems.at[2, j],
            device_id=sibling, device_id_type=MESH,
        )

    for j in range(2):
        own_tensor(j).start()
    small_copies = [
        pltpu.make_async_copy(source, target, small_sems.at[i])
        for i, (source, target) in enumerate(
            [
                (joining_ref, joining),
                (dims_ref, tables.at[state, pl.ds(2 * PHYS, 2)]),
                (coeff_ref, coeffs),
                (pattern_ref, pattern),
            ]
        )
    ]
    for copy in small_copies:
        copy.start()

    for d in range(CHIPS):
        if d not in HUBS:
            slot = at((4 - d // 32) % 4 * 32 + (8 - d // 4 % 8) % 8 * 4 + (4 - d % 4) % 4)
            gathered_even[slot] = jnp.zeros((PHYS, ROWS, COLS), jnp.bfloat16)
            gathered_odd[slot] = jnp.zeros((PHYS, ROWS, COLS), jnp.bfloat16)

    for copy in small_copies:
        copy.wait()

    turned = jnp.concatenate([joining[...], jnp.zeros((CHIPS - 2 * PHYS, CHIPS), jnp.int32)], axis=0).T
    left_ids = lax.broadcasted_iota(jnp.int32, (CHIPS, CHIPS), 0)
    right_ids = lax.broadcasted_iota(jnp.int32, (CHIPS, CHIPS), 1)
    for row in range(2 * PHYS):
        hit = jnp.where(turned[:, row : row + 1] == right_ids, left_ids, 0)
        tables[state, row : row + 1] = jnp.max(hit, axis=0, keepdims=True)
    weights_all[state, :, :PHYS] = coeffs[...] * pattern[...].astype(jnp.float32)

    def sent_table(slot):
        return pltpu.make_async_remote_copy(
            tables.at[slot], tables.at[slot], table_sems.at[0], table_sems.at[1],
            device_id=sibling, device_id_type=MESH,
        )

    def sent_weights(slot):
        return pltpu.make_async_remote_copy(
            weights_all.at[slot], weights_all.at[slot], table_sems.at[2], table_sems.at[3],
            device_id=sibling, device_id_type=MESH,
        )

    lookup_copy = pltpu.make_async_copy(tables, lookup, table_sems.at[4])
    start_copy.wait()
    pl.semaphore_wait(barrier, len(NEAR) + 1)

    for j in range(2):
        sent_tensor(j, state).start()
    sent_table(state).start()
    sent_weights(state).start()

    row_ids = (tile // 2) * ROWS + lax.broadcasted_iota(jnp.int32, (ROWS, COLS), 0)
    col_ids = (tile % 2) * COLS + lax.broadcasted_iota(jnp.int32, (ROWS, COLS), 1)

    def all_made(site):
        slots = pl.ds(0, TILES - 1)
        return pltpu.make_async_remote_copy(
            gathered_even.at[slots], gathered_even.at[slots], made_send.at[site], made_recv.at[site],
            device_id=sibling, device_id_type=MESH,
        )

    def all_joined(site):
        slots = pl.ds(0, CHIPS - 1)
        return pltpu.make_async_remote_copy(
            joined.at[0, slots], joined.at[0, slots], joined_send.at[site], joined_recv.at[site],
            device_id=sibling, device_id_type=MESH,
        )

    def part_copy():
        return pltpu.make_async_remote_copy(
            parting, out_ref.at[1], part_sems.at[0], part_sems.at[1],
            device_id=sibling, device_id_type=MESH,
        )

    def site_step(section, row, gathered):
        site = section * 2 + row

        @pl.when(section == state)
        def _():
            own_tensor(row).wait()

        @pl.when(section != state)
        def _():
            sent_tensor(row, 1 - state).wait_recv()

        for phys in range(PHYS):
            product = jnp.dot(remainder[...], tensors[site, phys], preferred_element_type=jnp.float32)
            for side in range(2):
                part = product[:, side * COLS : (side + 1) * COLS].reshape(B // ROWS, ROWS, COLS)
                made[site, :, side, phys] = part.astype(jnp.bfloat16)

        for d in HUBS:
            if d:
                hub_half = zs[d // 4 % 8] // 4
                hub_tile = ((xs[d // 32] + 2 * hub_half) % 4 * 4 + zs[d // 4 % 8] % 4) * 4 + (ys[d % 4] + 2 * hub_half) % 4
                pltpu.make_async_remote_copy(
                    made.at[site, hub_tile // 2, hub_tile % 2], gathered.at[me],
                    made_send.at[site], made_recv.at[site],
                    device_id={"blk": at(d)}, device_id_type=MESH,
                ).start()
        own = pltpu.make_async_copy(made.at[site, tile // 2, tile % 2], gathered.at[me], own_sem.at[0])
        own.start()

        if row == 0:
            @pl.when(section == 0)
            def _():
                sent_table(1 - state).wait_recv()
                sent_weights(1 - state).wait_recv()
                lookup_copy.start()
                lookup_copy.wait()

        own.wait()
        all_made(site).wait_recv()
        weight_row = weights_all[section, row : row + 1]
        weights = [weight_row[:, phys : phys + 1] for phys in range(PHYS)]

        crossing = (1 - state) * section * row
        core, lane = state + crossing, site + crossing
        for d in ORDER:
            chip = at(d)
            total = jnp.zeros((ROWS, COLS), jnp.float32)
            for phys in range(PHYS):
                left = lookup[section, row * PHYS + phys, chip]
                total = total + weights[phys] * gathered[left, phys].astype(jnp.float32)
            size = lookup[section, 2 * PHYS + row, chip]
            total = jnp.where((row_ids < size) & (col_ids < size), total, 0.0)
            joined[site, chip] = total.astype(jnp.bfloat16)
            if d:
                pltpu.make_async_remote_copy(
                    joined.at[site, chip], returned.at[site, state, half, tile],
                    joined_send.at[lane], joined_recv.at[lane],
                    device_id={"sect": core, "blk": chip}, device_id_type=MESH,
                ).start()

        def finish(held):
            tiles = returned[site, held, 0].astype(jnp.float32) + returned[site, held, 1].astype(jnp.float32)
            squares = jnp.sum(tiles * tiles, axis=0)
            meansq = jnp.sum(squares, keepdims=True) * (1.0 / (B * B))
            scale = lax.rsqrt(meansq + 1e-06)
            tiles = (tiles * scale[None]).reshape(B // ROWS, 2, ROWS, COLS)
            for side in range(2):
                part = tiles[:, side].reshape(B, COLS).astype(jnp.bfloat16)
                remainder[:, side * COLS : (side + 1) * COLS] = part

        def to_sibling():
            return pltpu.make_async_remote_copy(
                joined.at[site, me], returned.at[site, state, half, tile],
                part_sems.at[2], part_sems.at[3], device_id=sibling, device_id_type=MESH,
            )

        def keep_own():
            own = pltpu.make_async_copy(joined.at[site, me], returned.at[site, state, half, tile], own_sem.at[0])
            own.start()
            own.wait()
            all_joined(site).wait_recv()
            finish(state)

        if row == 0:
            keep_own()
        else:
            @pl.when((section == 0) | (state == 1))
            def _():
                keep_own()

            @pl.when((section == 0) & (state == 0))
            def _():
                out_ref[0] = remainder[...]

            @pl.when((section == 0) & (state == 1))
            def _():
                parting[...] = remainder[...]
                part_copy().start()

            @pl.when((section == 1) & (state == 0))
            def _():
                to_sibling().start()
                to_sibling().wait_send()

            @pl.when((section == 1) & (state == 1))
            def _():
                out_ref[1] = remainder[...]
                to_sibling().wait_recv()
                all_joined(SITES).wait_recv()
                finish(0)
                out_ref[0] = remainder[...]

    def section_step(section, carry):
        site_step(section, 0, gathered_even)
        site_step(section, 1, gathered_odd)
        return carry

    lax.fori_loop(0, SITES // 2, section_step, 0)

    for j in range(2):
        sent_tensor(j, state).wait_send()
    sent_table(state).wait_send()
    sent_weights(state).wait_send()

    def settle(site, carry):
        all_made(site).wait_send()
        all_joined(site + (1 - state) * (site // (SITES - 1))).wait_send()
        return carry

    lax.fori_loop(0, SITES, settle, 0)

    @pl.when(state == 1)
    def _():
        part_copy().wait_send()

    @pl.when(state == 0)
    def _():
        part_copy().wait_recv()


def shards(start_remainders, site_tensors, mpo_coeffs, mpo_pattern, joining, sector_dims):
    bf16, dma = jnp.bfloat16, pltpu.SemaphoreType.DMA
    out = pl.pallas_call(
        kernel,
        out_shape=jax.ShapeDtypeStruct((2, B, B), bf16),
        in_specs=[pl.BlockSpec(memory_space=pltpu.HBM)] * 6,
        out_specs=pl.BlockSpec(memory_space=pltpu.VMEM),
        scratch_shapes=[
            pltpu.VMEM((2, PHYS), jnp.float32),
            pltpu.VMEM((2, PHYS), jnp.int32),
            pltpu.VMEM((2 * PHYS, CHIPS), jnp.int32),
            pltpu.VMEM((2, 16, CHIPS), jnp.int32),
            pltpu.VMEM((2, 2, CHIPS), jnp.float32),
            pltpu.SMEM((2, 16, CHIPS), jnp.int32),
            pltpu.VMEM((SITES, PHYS, B, B), bf16),
            pltpu.VMEM((B, B), bf16),
            pltpu.VMEM((B, B), bf16),
            pltpu.VMEM((SITES, B // ROWS, 2, PHYS, ROWS, COLS), bf16),
            pltpu.VMEM((CHIPS, PHYS, ROWS, COLS), bf16),
            pltpu.VMEM((CHIPS, PHYS, ROWS, COLS), bf16),
            pltpu.VMEM((SITES, CHIPS, ROWS, COLS), bf16),
            pltpu.VMEM((SITES, 2, 2, TILES, ROWS, COLS), bf16),
            dma((3, 2)),
            dma((SITES,)),
            dma((SITES,)),
            dma((SITES + 1,)),
            dma((SITES + 1,)),
            dma((2,)),
            dma((4,)),
            dma((5,)),
            dma((4,)),
        ],
        compiler_params=pltpu.CompilerParams(
            collective_id=0, has_side_effects=True, vmem_limit_bytes=63 << 20
        ),
        name="zip_up",
    )(
        start_remainders[:, 0],
        site_tensors[:, 0],
        mpo_coeffs,
        mpo_pattern,
        joining.reshape(2 * PHYS, CHIPS),
        sector_dims,
    )
    return out[None, :, None]


def solution(mesh):
    in_specs = (
        P(None, "blk", None, None),
        P("sect", "blk", None, None, None),
        P("sect", None),
        P("sect", None),
        P("sect", None, None),
        P("sect", None),
    )
    out_specs = P("sect", None, "blk", None, None)
    return jax.shard_map(shards, mesh=mesh, in_specs=in_specs, out_specs=out_specs, check_vma=False)
```

```python
import jax
import jax.numpy as jnp
from jax import lax
from jax.experimental import pallas as pl
from jax.experimental.pallas import tpu as pltpu
from jax.sharding import PartitionSpec as P

MESH = pl.DeviceIdType.MESH
B = 256
PHYS = 4
SITES = 4
CHIPS = 128
TILES = 64
ROWS, COLS = 8, 128
def hops(d):
    return min(d // 32, 4 - d // 32) + min(d // 4 % 8, 8 - d // 4 % 8) + min(d % 4, 4 - d % 4)


def alternate():
    chosen = []
    for d in sorted(range(CHIPS), key=lambda d: (-hops(d), d * 75 % CHIPS)):
        back = (4 - d // 32) % 4 * 32 + (8 - d // 4 % 8) % 8 * 4 + (4 - d % 4) % 4
        chosen += [e for e in (d, back) if e not in chosen]
    return [e for i, e in enumerate(chosen) if e not in chosen[:i]]


ORDER = alternate()
NEAR = [d for d in ORDER if 0 < hops(d) <= 4]


def nearer_hubs():
    chosen = []
    for d in range(CHIPS):
        opposite = (d // 32 + 2) % 4 * 32 + (d // 4 % 8 + 4) % 8 * 4 + (d % 4 + 2) % 4
        here, there = [(hops(e), min(e // 4 % 8, 8 - e // 4 % 8)) for e in (d, opposite)]
        tie = here == there and d in (10, 26, 41, 59, 107, 121)
        if here < there or tie:
            chosen.append(d)
    return [d for d in ORDER if d in chosen]


HUBS = nearer_hubs()


def kernel(
    start_ref, tensor_ref, coeff_ref, pattern_ref, joining_ref, dims_ref, out_ref,
    coeffs, pattern, joining, tables, weights_all, lookup,
    tensors, remainder, parting, made, gathered_even, gathered_odd, joined, returned,
    tensor_sems, made_send, made_recv, joined_send, joined_recv, own_sem, part_sems, table_sems, small_sems,
):
    me, state = lax.axis_index("blk"), lax.axis_index("sect")
    x, z, y = me // 32, (me // 4) % 8, me % 4
    sibling = {"sect": 1 - state}
    half = z // 4
    tile = ((x + 2 * half) % 4 * 4 + z % 4) * 4 + (y + 2 * half) % 4
    way = 1 - 2 * state
    xs = [(x + 4 + way * i) % 4 for i in range(4)]
    zs = [(z + 8 + way * i) % 8 for i in range(8)]
    ys = [(y + 4 + way * i) % 4 for i in range(4)]

    def at(d):
        return xs[d // 32] * 32 + zs[d // 4 % 8] * 4 + ys[d % 4]

    barrier = pltpu.get_barrier_semaphore()
    pl.semaphore_signal(barrier, inc=1, device_id=sibling, device_id_type=MESH)

    for d in NEAR:
        pl.semaphore_signal(barrier, inc=1, device_id={"blk": at(d)}, device_id_type=MESH)

    start_copy = pltpu.make_async_copy(start_ref.at[state], remainder, own_sem.at[1])
    start_copy.start()

    def own_tensor(j):
        return pltpu.make_async_copy(tensor_ref.at[j], tensors.at[state * 2 + j], tensor_sems.at[0, j])

    def sent_tensor(j, slot):
        return pltpu.make_async_remote_copy(
            tensor_ref.at[j], tensors.at[slot * 2 + j], tensor_sems.at[1, j], tensor_sems.at[2, j],
            device_id=sibling, device_id_type=MESH,
        )

    for j in range(2):
        own_tensor(j).start()
    small_copies = [
        pltpu.make_async_copy(source, target, small_sems.at[i])
        for i, (source, target) in enumerate(
            [
                (joining_ref, joining),
                (dims_ref, tables.at[state, pl.ds(2 * PHYS, 2)]),
                (coeff_ref, coeffs),
                (pattern_ref, pattern),
            ]
        )
    ]
    for copy in small_copies:
        copy.start()

    for d in range(CHIPS):
        if d not in HUBS:
            slot = at((4 - d // 32) % 4 * 32 + (8 - d // 4 % 8) % 8 * 4 + (4 - d % 4) % 4)
            gathered_even[slot] = jnp.zeros((PHYS, ROWS, COLS), jnp.bfloat16)
            gathered_odd[slot] = jnp.zeros((PHYS, ROWS, COLS), jnp.bfloat16)

    for copy in small_copies:
        copy.wait()

    turned = jnp.concatenate([joining[...], jnp.zeros((CHIPS - 2 * PHYS, CHIPS), jnp.int32)], axis=0).T
    left_ids = lax.broadcasted_iota(jnp.int32, (CHIPS, CHIPS), 0)
    right_ids = lax.broadcasted_iota(jnp.int32, (CHIPS, CHIPS), 1)
    for row in range(2 * PHYS):
        hit = jnp.where(turned[:, row : row + 1] == right_ids, left_ids, 0)
        tables[state, row : row + 1] = jnp.max(hit, axis=0, keepdims=True)
    weights_all[state, :, :PHYS] = coeffs[...] * pattern[...].astype(jnp.float32)

    def sent_table(slot):
        return pltpu.make_async_remote_copy(
            tables.at[slot], tables.at[slot], table_sems.at[0], table_sems.at[1],
            device_id=sibling, device_id_type=MESH,
        )

    def sent_weights(slot):
        return pltpu.make_async_remote_copy(
            weights_all.at[slot], weights_all.at[slot], table_sems.at[2], table_sems.at[3],
            device_id=sibling, device_id_type=MESH,
        )

    lookup_copy = pltpu.make_async_copy(tables, lookup, table_sems.at[4])
    start_copy.wait()
    pl.semaphore_wait(barrier, len(NEAR) + 1)

    for j in range(2):
        sent_tensor(j, state).start()
    sent_table(state).start()
    sent_weights(state).start()

    row_ids = (tile // 2) * ROWS + lax.broadcasted_iota(jnp.int32, (ROWS, COLS), 0)
    col_ids = (tile % 2) * COLS + lax.broadcasted_iota(jnp.int32, (ROWS, COLS), 1)

    def all_made(site):
        slots = pl.ds(0, TILES - 1)
        return pltpu.make_async_remote_copy(
            gathered_even.at[slots], gathered_even.at[slots], made_send.at[site], made_recv.at[site],
            device_id=sibling, device_id_type=MESH,
        )

    def all_joined(site):
        slots = pl.ds(0, CHIPS - 1)
        return pltpu.make_async_remote_copy(
            joined.at[0, slots], joined.at[0, slots], joined_send.at[site], joined_recv.at[site],
            device_id=sibling, device_id_type=MESH,
        )

    def part_copy():
        return pltpu.make_async_remote_copy(
            parting, out_ref.at[1], part_sems.at[0], part_sems.at[1],
            device_id=sibling, device_id_type=MESH,
        )

    def site_step(section, row, gathered):
        site = section * 2 + row

        @pl.when(section == state)
        def _():
            own_tensor(row).wait()

        @pl.when(section != state)
        def _():
            sent_tensor(row, 1 - state).wait_recv()

        for phys in range(PHYS):
            product = jnp.dot(remainder[...], tensors[site, phys], preferred_element_type=jnp.float32)
            for side in range(2):
                part = product[:, side * COLS : (side + 1) * COLS].reshape(B // ROWS, ROWS, COLS)
                made[site, :, side, phys] = part.astype(jnp.bfloat16)

        for d in HUBS:
            if d:
                hub_half = zs[d // 4 % 8] // 4
                hub_tile = ((xs[d // 32] + 2 * hub_half) % 4 * 4 + zs[d // 4 % 8] % 4) * 4 + (ys[d % 4] + 2 * hub_half) % 4
                pltpu.make_async_remote_copy(
                    made.at[site, hub_tile // 2, hub_tile % 2], gathered.at[me],
                    made_send.at[site], made_recv.at[site],
                    device_id={"blk": at(d)}, device_id_type=MESH,
                ).start()
        own = pltpu.make_async_copy(made.at[site, tile // 2, tile % 2], gathered.at[me], own_sem.at[0])
        own.start()

        if row == 0:
            @pl.when(section == 0)
            def _():
                sent_table(1 - state).wait_recv()
                sent_weights(1 - state).wait_recv()
                lookup_copy.start()
                lookup_copy.wait()

        own.wait()
        all_made(site).wait_recv()
        weight_row = weights_all[section, row : row + 1]
        weights = [weight_row[:, phys : phys + 1] for phys in range(PHYS)]

        crossing = (1 - state) * section * row
        core, lane = state + crossing, site + crossing
        for d in ORDER:
            chip = at(d)
            total = jnp.zeros((ROWS, COLS), jnp.float32)
            for phys in range(PHYS):
                left = lookup[section, row * PHYS + phys, chip]
                total = total + weights[phys] * gathered[left, phys].astype(jnp.float32)
            size = lookup[section, 2 * PHYS + row, chip]
            total = jnp.where((row_ids < size) & (col_ids < size), total, 0.0)
            joined[site, chip] = total.astype(jnp.bfloat16)
            if d:
                pltpu.make_async_remote_copy(
                    joined.at[site, chip], returned.at[site, state, half, tile],
                    joined_send.at[lane], joined_recv.at[lane],
                    device_id={"sect": core, "blk": chip}, device_id_type=MESH,
                ).start()

        def finish(held):
            tiles = returned[site, held, 0].astype(jnp.float32) + returned[site, held, 1].astype(jnp.float32)
            squares = jnp.sum(tiles * tiles, axis=0)
            meansq = jnp.sum(squares, keepdims=True) * (1.0 / (B * B))
            scale = lax.rsqrt(meansq + 1e-06)
            tiles = (tiles * scale[None]).reshape(B // ROWS, 2, ROWS, COLS)
            for side in range(2):
                part = tiles[:, side].reshape(B, COLS).astype(jnp.bfloat16)
                remainder[:, side * COLS : (side + 1) * COLS] = part

        def to_sibling():
            return pltpu.make_async_remote_copy(
                joined.at[site, me], returned.at[site, state, half, tile],
                part_sems.at[2], part_sems.at[3], device_id=sibling, device_id_type=MESH,
            )

        def keep_own():
            own = pltpu.make_async_copy(joined.at[site, me], returned.at[site, state, half, tile], own_sem.at[0])
            own.start()
            own.wait()
            all_joined(site).wait_recv()
            finish(state)

        if row == 0:
            keep_own()
        else:
            @pl.when((section == 0) | (state == 1))
            def _():
                keep_own()

            @pl.when((section == 0) & (state == 0))
            def _():
                out_ref[0] = remainder[...]

            @pl.when((section == 0) & (state == 1))
            def _():
                parting[...] = remainder[...]
                part_copy().start()

            @pl.when((section == 1) & (state == 0))
            def _():
                to_sibling().start()
                to_sibling().wait_send()

            @pl.when((section == 1) & (state == 1))
            def _():
                out_ref[1] = remainder[...]
                to_sibling().wait_recv()
                all_joined(SITES).wait_recv()
                finish(0)
                out_ref[0] = remainder[...]

    def section_step(section, carry):
        site_step(section, 0, gathered_even)
        site_step(section, 1, gathered_odd)
        return carry

    lax.fori_loop(0, SITES // 2, section_step, 0)

    for j in range(2):
        sent_tensor(j, state).wait_send()
    sent_table(state).wait_send()
    sent_weights(state).wait_send()

    def settle(site, carry):
        all_made(site).wait_send()
        all_joined(site + (1 - state) * (site // (SITES - 1))).wait_send()
        return carry

    lax.fori_loop(0, SITES, settle, 0)

    @pl.when(state == 1)
    def _():
        part_copy().wait_send()

    @pl.when(state == 0)
    def _():
        part_copy().wait_recv()


def shards(start_remainders, site_tensors, mpo_coeffs, mpo_pattern, joining, sector_dims):
    bf16, dma = jnp.bfloat16, pltpu.SemaphoreType.DMA
    out = pl.pallas_call(
        kernel,
        out_shape=jax.ShapeDtypeStruct((2, B, B), bf16),
        in_specs=[pl.BlockSpec(memory_space=pltpu.HBM)] * 6,
        out_specs=pl.BlockSpec(memory_space=pltpu.VMEM),
        scratch_shapes=[
            pltpu.VMEM((2, PHYS), jnp.float32),
            pltpu.VMEM((2, PHYS), jnp.int32),
            pltpu.VMEM((2 * PHYS, CHIPS), jnp.int32),
            pltpu.VMEM((2, 16, CHIPS), jnp.int32),
            pltpu.VMEM((2, 2, CHIPS), jnp.float32),
            pltpu.SMEM((2, 16, CHIPS), jnp.int32),
            pltpu.VMEM((SITES, PHYS, B, B), bf16),
            pltpu.VMEM((B, B), bf16),
            pltpu.VMEM((B, B), bf16),
            pltpu.VMEM((SITES, B // ROWS, 2, PHYS, ROWS, COLS), bf16),
            pltpu.VMEM((CHIPS, PHYS, ROWS, COLS), bf16),
            pltpu.VMEM((CHIPS, PHYS, ROWS, COLS), bf16),
            pltpu.VMEM((SITES, CHIPS, ROWS, COLS), bf16),
            pltpu.VMEM((SITES, 2, 2, TILES, ROWS, COLS), bf16),
            dma((3, 2)),
            dma((SITES,)),
            dma((SITES,)),
            dma((SITES + 1,)),
            dma((SITES + 1,)),
            dma((2,)),
            dma((4,)),
            dma((5,)),
            dma((4,)),
        ],
        compiler_params=pltpu.CompilerParams(
            collective_id=0, has_side_effects=True, vmem_limit_bytes=63 << 20
        ),
        name="zip_up",
    )(
        start_remainders[:, 0],
        site_tensors[:, 0],
        mpo_coeffs,
        mpo_pattern,
        joining.reshape(2 * PHYS, CHIPS),
        sector_dims,
    )
    return out[None, :, None]


def solution(mesh):
    in_specs = (
        P(None, "blk", None, None),
        P("sect", "blk", None, None, None),
        P("sect", None),
        P("sect", None),
        P("sect", None, None),
        P("sect", None),
    )
    out_specs = P("sect", None, "blk", None, None)
    return jax.shard_map(shards, mesh=mesh, in_specs=in_specs, out_specs=out_specs, check_vma=False)
```
